32 devices in a mesh: cls: 4 (over z), col: 8 (over y, x, core).
Axes of the slice: x: 2, y: 2, z: 4, core: 2. Of those that a mesh axis runs over, the one named last changes fastest.
Arguments:
- coeffs_t: float32 [49152, 1024], P(('cls', 'col')), may hold values from -6 to 6
- alpha_table: float32 [64, 4096], replicated, may hold values from -0.1875 to 0.1875
- alpha_blocks: int32 [16, 16], replicated, may hold values from 0 to 15, all different within a row
- alpha_types: int32 [16, 16], replicated, may hold values from 0 to 63
- beta_table: float32 [64, 4096], replicated, may hold values from -0.21875 to 0.21875
- beta_blocks: int32 [768, 12], P('cls'), may hold values from 0 to 383, all different within a row
- beta_types: int32 [768, 12], P('cls'), may hold values from 0 to 63
- row_counts: int32 [8], replicated, may hold values from 1 to 192, 1024 in all
Outputs:
- sigma_slots: float32 [1536, 49152], P('col', 'cls')
The draws below stay inside these ranges and needn't reach their ends.
Inputs may be any that keep to these rules, and one draw needn't show every extreme that they name: `alpha_blocks`: each row names 16 different alpha blocks. `beta_blocks`: each row names 12 different entries: below 192 a block of the own class, from 192 on a block of the partner class. `row_counts`: the counts sum to 1024 and the largest is exactly 192.
All inputs are finite; a program needn't handle non-finite values.
Results may differ from the reference program's by a relative error of at most 0.0003.
Values sent between devices are 32-bit elements; how exact they have to be, the bound alone decides.
A program may use at most 128 MiB of HBM per device.

```python
import math
import jax
import jax.numpy as jnp
import numpy as np
from jax import lax

NA = 1024
NB = 49152
BLOCK = 64
ALPHA_K = 16
BETA_K = 12
TYPES = 64
NAB = 16
NBB = 768
NBC = 192
CAP = 192
N_CLS = 4
N_COL = 8


def place_ends(array, own_key, least, top_value):
    index_at = [jax.random.randint(jax.random.fold_in(own_key, axis), (), 0, length) for axis, length in enumerate(array.shape)]
    widest = array.shape.index(max(array.shape))
    beside = index_at[:widest] + [(index_at[widest] + 1) % array.shape[widest]] + index_at[widest + 1:]
    return array.at[tuple(index_at)].set(least).at[tuple(beside)].set(top_value)


def block_levels(own_key, dims, shards, least, top_value):
    def one(dim, parts):
        steps = jax.random.uniform(jax.random.fold_in(jax.random.fold_in(own_key, 6), dim), (parts,), jnp.float32, least / len(shards), top_value / len(shards))
        return jnp.repeat(jnp.exp(steps), dims[dim] // parts).reshape((-1,) + (1,) * (len(dims) - dim - 1))

    gain = one(*shards[0])
    for cut in shards[1:]:
        gain = gain * one(*cut)
    return gain


def different_ones(rng, rows, number_of, top, lift):
    sequence = jax.random.permutation(jax.random.fold_in(rng, 1), number_of)
    favour = sequence
    for power in range(3):
        favour = favour * favour // number_of
    favour = favour * lift // number_of
    chance = jax.random.randint(jax.random.fold_in(rng, 2), (rows, number_of), 0, 4096) + favour
    holders = jax.random.permutation(jax.random.fold_in(rng, 3), rows)[jnp.arange(number_of) % rows]
    chance = jnp.where(jnp.arange(rows)[:, None] == holders[None, :], 1 << 14, chance)
    priority = chance * number_of + jnp.arange(number_of)
    return lax.top_k(priority.astype(jnp.int32), top)[1].astype(jnp.int32)


def length_profile(number_of, total, reach, slope):
    loads = [(1 << 20) // math.isqrt(rank ** slope) + 1 for rank in range(2, number_of + 1)]
    spare, holding = total - reach - (number_of - 1), [1] * (number_of - 1)
    while spare > 0:
        movable = [i for i in range(number_of - 1) if holding[i] < reach]
        whole, budget = sum([loads[i] for i in movable]), spare
        for i in movable:
            more = min(reach - holding[i], max(1, budget * loads[i] // whole), spare)
            holding[i] = holding[i] + more
            spare = spare - more
    return np.array([reach] + holding)


def ragged_sizes(stream_key, count, total, reach, lean):
    if count == 2:
        one = jax.random.randint(stream_key, (), max(1, total - reach), min(reach, total - 1) + 1)
        return jnp.stack([one, total - one])
    sizes = jnp.asarray(length_profile(count, total, reach, lean), jnp.int32)
    pairs = (count - 1) // 2
    source_of, taker = sizes[1:1 + 2 * pairs:2], sizes[2:2 + 2 * pairs:2]
    slack = jnp.minimum(source_of - 1, reach - taker)
    moved = jax.random.randint(jax.random.fold_in(stream_key, 1), (pairs,), 0, 1 << 20) % (slack + 1)
    sizes = sizes.at[1:1 + 2 * pairs:2].set(source_of - moved).at[2:2 + 2 * pairs:2].set(taker + moved)
    return sizes[jax.random.permutation(jax.random.fold_in(stream_key, 2), count)]


def bell_draw(rng, extent, spread, bound, split=(), kind=jnp.bfloat16):
    gain = block_levels(rng, extent, split, -0.22, 0.18) if split else 1.0
    result = jax.random.normal(rng, extent, jnp.float32) * spread * gain
    return jnp.minimum(jnp.maximum(result, -bound), bound).astype(kind)


def setup_inputs(seed: int = 0) -> dict:
    key_of = jax.random.split(jax.random.key(seed), 9)
    coeffs_t = bell_draw(key_of[0], (NB, NA), 1.0, 6.0, ((0, 32),), jnp.float32)
    alpha_table = bell_draw(key_of[1], (TYPES, BLOCK * BLOCK), (BLOCK * ALPHA_K) ** -0.5, 0.1875, (), jnp.float32)
    alpha_blocks = different_ones(key_of[2], NAB, NAB, ALPHA_K, 0)
    alpha_types = place_ends(jax.random.randint(key_of[3], (NAB, ALPHA_K), 0, TYPES), jax.random.fold_in(key_of[3], 1), 0, TYPES - 1).astype(jnp.int32)
    beta_table = bell_draw(key_of[4], (TYPES, BLOCK * BLOCK), (BLOCK * BETA_K) ** -0.5, 0.21875, (), jnp.float32)
    beta_blocks = different_ones(key_of[5], NBB, 2 * NBC, BETA_K, 0)
    beta_types = place_ends(jax.random.randint(key_of[6], (NBB, BETA_K), 0, TYPES), jax.random.fold_in(key_of[6], 1), 0, TYPES - 1).astype(jnp.int32)
    row_counts = ragged_sizes(key_of[7], N_COL, NA, CAP, 1).astype(jnp.int32)
    return dict(coeffs_t=coeffs_t, alpha_table=alpha_table, alpha_blocks=alpha_blocks, alpha_types=alpha_types, beta_table=beta_table, beta_blocks=beta_blocks, beta_types=beta_types, row_counts=row_counts)


exact_mode = lax.Precision.HIGHEST


def alpha_product(coeffs, alpha_table, alpha_blocks, alpha_types):
    blocked = coeffs.reshape(NA // BLOCK, BLOCK, NB)
    tables = alpha_table.reshape(TYPES, BLOCK, BLOCK)

    def one_block(block_id):
        source = jnp.take(blocked, alpha_blocks[block_id], axis=0)
        matrices = jnp.take(tables, alpha_types[block_id], axis=0)
        return jnp.einsum("kab,kbn->an", matrices, source, precision=exact_mode)

    results = lax.map(one_block, jnp.arange(NA // BLOCK, dtype=jnp.int32))
    return results.reshape(NA, NB)


def beta_product(coeffs, beta_table, beta_blocks, beta_types):
    per_class = NB // (BLOCK * N_CLS)
    blocked = coeffs.reshape(NA, NB // BLOCK, BLOCK)
    tables = beta_table.reshape(TYPES, BLOCK, BLOCK)

    def one_block(block_id):
        own_class = (block_id // per_class).astype(jnp.int32)
        other_class = jnp.bitwise_xor(own_class, 1).astype(jnp.int32)
        entries = beta_blocks[block_id]
        class_of = jnp.where(entries < per_class, own_class, other_class)
        global_id = (class_of * per_class + entries % per_class).astype(jnp.int32)
        source = jnp.take(blocked, global_id, axis=1)
        matrices = jnp.take(tables, beta_types[block_id], axis=0)
        return jnp.einsum("rka,kab->rb", source, matrices, precision=exact_mode)

    results = lax.map(one_block, jnp.arange(NB // BLOCK, dtype=jnp.int32))
    return jnp.transpose(results, (1, 0, 2)).reshape(NA, NB)


def reference(coeffs_t, alpha_table, alpha_blocks, alpha_types, beta_table, beta_blocks, beta_types, row_counts):
    coeffs = jnp.transpose(coeffs_t)
    sigma_total = alpha_product(coeffs, alpha_table, alpha_blocks, alpha_types)
    sigma_total = sigma_total + beta_product(coeffs, beta_table, beta_blocks, beta_types)
    starts = (jnp.cumsum(row_counts) - row_counts).astype(jnp.int32)
    offsets = jnp.arange(CAP, dtype=jnp.int32)
    row_index = (starts[:, None] + offsets[None, :]).reshape(-1).astype(jnp.int32)
    padded = jnp.concatenate([sigma_total, jnp.zeros((CAP, NB), jnp.float32)], 0)
    slot_rows = jnp.take(padded, row_index, axis=0)
    in_range = (offsets[None, :] < row_counts[:, None]).reshape(-1)
    return jnp.where(in_range[:, None], slot_rows, jnp.float32(0.0))
```

```python
import functools

import jax
import jax.numpy as jnp
from jax import lax
from jax.experimental import pallas as pl
from jax.experimental.pallas import tpu as pltpu
from jax.sharding import PartitionSpec as P

ROW_PARTS = 3
TILE = 8
VMEM_BYTES = 56 * 1024 * 1024


def swapped(block, axis, apart):
    count = lax.axis_size(axis)
    route = []
    for low in range(count):
        high = low | 1 << apart
        if high != low and high < count:
            route += [(low, high), (high, low)]
    return lax.ppermute(block, axis, route)


def split_outside(x):
    high = lax.reduce_precision(x, 8, 7)
    return high.astype(jnp.bfloat16), (x - high).astype(jnp.bfloat16)


def split_inside(x):
    high = x.astype(jnp.bfloat16)
    return high, (x - high.astype(jnp.float32)).astype(jnp.bfloat16)


def column_chunk(width):
    for chunk in (512, 384, 256, 128):
        if width % chunk == 0:
            return chunk
    return width


def write_slots(starts, tall, out_refs):
    parts = len(out_refs)
    piece = out_refs[0].shape[1]
    for slot in range(out_refs[0].shape[0]):
        for part in range(parts):
            first = starts[slot] + part * piece
            shift = lax.rem(first, TILE)
            span = piece + TILE
            rows = pl.ds(pl.multiple_of(first - shift, TILE), span)
            moved = pltpu.roll(tall[rows, :], lax.rem(span - shift, span), 0)
            out_refs[part][slot] = moved[:piece]


def coeff_kernel(starts, coeffs, *rest):
    out_refs, tall = rest[:-1], rest[-1]
    rows = coeffs.shape[1]
    tall[:rows, :] = coeffs[...].T
    tall[rows:, :] = jnp.zeros((tall.shape[0] - rows, tall.shape[1]), jnp.float32)
    write_slots(starts, tall, out_refs)


def alpha_kernel(starts, coeffs, high_ref, low_ref, out_ref, tall):
    rows = coeffs.shape[1]
    c_high, c_low = split_inside(coeffs[...])
    dot = functools.partial(
        lax.dot_general,
        dimension_numbers=(((1,), (1,)), ((), ())),
        preferred_element_type=jnp.float32,
    )
    tall[:rows, :] = (dot(low_ref[...], c_high) + dot(high_ref[...], c_low)) + dot(
        high_ref[...], c_high
    )
    tall[rows:, :] = jnp.zeros((tall.shape[0] - rows, tall.shape[1]), jnp.float32)
    write_slots(starts, tall, [out_ref])


def slots_call(kernel, coeffs_t, starts, matrices, groups, capacity, parts, name):
    width, rows = coeffs_t.shape
    chunk = column_chunk(width)
    piece = capacity // parts
    out = jax.ShapeDtypeStruct((groups, piece, width), jnp.float32)
    return pl.pallas_call(
        kernel,
        out_shape=[out] * parts,
        grid=(width // chunk,),
        in_specs=[
            pl.BlockSpec(memory_space=pltpu.SMEM),
            pl.BlockSpec((chunk, rows), lambda i: (i, 0)),
        ]
        + [pl.BlockSpec(m.shape, lambda i: (0, 0)) for m in matrices],
        out_specs=[pl.BlockSpec((groups, piece, chunk), lambda i: (0, 0, i))] * parts,
        scratch_shapes=[pltpu.VMEM((rows + capacity + TILE, chunk), jnp.float32)],
        compiler_params=pltpu.CompilerParams(vmem_limit_bytes=VMEM_BYTES),
        name=name,
    )(starts, coeffs_t, *matrices)


def beta_kernel(steps, parts, block, keep, entries, types, *rest):
    own, partner = rest[:parts], rest[parts : 2 * parts]
    alpha, left, right, out, x_high, x_low = rest[2 * parts :]
    step = pl.program_id(0)
    width = alpha.shape[2]
    per_row = entries.shape[0] // (x_high.shape[0] // (2 * block))

    def store(pieces, at):
        tall = jnp.concatenate([piece[0] for piece in pieces], 0) if parts > 1 else pieces[0][0]
        high, low = split_inside(tall.T)
        rows = pl.ds(pl.multiple_of(at * width, block), width)
        x_high[rows, :] = high
        x_low[rows, :] = low

    @pl.when(step < steps)
    def _():
        store(own, step)

    @pl.when(jnp.logical_and(step >= steps, step < 2 * steps))
    def _():
        store(partner, step)

    def one(m):
        base = m * per_row
        places = [
            pl.ds(pl.multiple_of(entries[base + k] * block, block), block) for k in range(per_row)
        ]
        weights = jnp.concatenate(
            [
                left[types[base + k]] + right[types[base + k + 1]]
                for k in range(0, per_row, 2)
            ],
            1,
        )
        high = jnp.concatenate([x_high[place, :] for place in places], 0)
        low = jnp.concatenate([x_low[place, :] for place in places], 0)
        both = jnp.dot(weights, high, preferred_element_type=jnp.float32)
        cross = jnp.dot(weights[:block], low, preferred_element_type=jnp.float32)
        return both[:block] + (both[block:] + cross)

    @pl.when(step >= 2 * steps)
    def _():
        first = (step - 2 * steps) * (width // block)
        row = lax.broadcasted_iota(jnp.int32, (out.shape[0], 2 * block), 0)
        kept = row < keep[0]

        def pair(at, carry):
            m = first + 2 * at
            tall = jnp.concatenate([one(m), one(m + 1)], 0)
            lanes = pl.ds(pl.multiple_of(at * (2 * block), 2 * block), 2 * block)
            total = tall.T + alpha[0, :, lanes]
            out[:, lanes] = jnp.where(kept, total, jnp.float32(0.0))
            return carry

        lax.fori_loop(0, width // (2 * block), pair, 0)


def beta_call(own, partner, alpha, left, right, entries, types, keep, block):
    groups, capacity, width = alpha.shape
    parts = len(own)
    piece = capacity // parts
    whole = lambda a: pl.BlockSpec(a.shape, lambda i: (0, 0, 0))
    smem = pl.BlockSpec(memory_space=pltpu.SMEM)

    def at(offset):
        return lambda i: (jnp.clip(i - offset, 0, groups - 1), 0, 0)

    return pl.pallas_call(
        functools.partial(beta_kernel, groups, parts, block),
        out_shape=jax.ShapeDtypeStruct((capacity, groups * width), jnp.float32),
        grid=(3 * groups,),
        in_specs=[smem, smem, smem]
        + [pl.BlockSpec((1, piece, width), at(0))] * parts
        + [pl.BlockSpec((1, piece, width), at(groups))] * parts
        + [pl.BlockSpec((1, capacity, width), at(2 * groups)), whole(left), whole(right)],
        out_specs=pl.BlockSpec(
            (capacity, width), lambda i: (0, jnp.clip(i - 2 * groups, 0, groups - 1))
        ),
        scratch_shapes=[pltpu.VMEM((2 * groups * width, capacity), jnp.bfloat16)] * 2,
        compiler_params=pltpu.CompilerParams(vmem_limit_bytes=VMEM_BYTES),
        name="beta_sum",
    )(keep, entries, types, *own, *partner, alpha, left, right)


def alpha_matrix(alpha_table, alpha_blocks, alpha_types, block):
    count = alpha_blocks.shape[0]
    hit = alpha_blocks[:, :, None] == jnp.arange(count, dtype=jnp.int32)[None, None, :]
    type_of = jnp.sum(jnp.where(hit, alpha_types[:, :, None], 0), 1)
    matrices = jnp.take(alpha_table, type_of, axis=0)
    matrices = jnp.where(jnp.any(hit, 1)[:, :, None], matrices, jnp.float32(0.0))
    matrices = matrices.reshape(count, count, block, block)
    return jnp.transpose(matrices, (0, 2, 1, 3)).reshape(count * block, count * block)


def beta_weights(beta_table, block):
    tables = jnp.transpose(beta_table.reshape(-1, block, block), (0, 2, 1))
    both = jnp.concatenate(split_outside(tables), 1)
    return (
        jnp.pad(both, ((0, 0), (0, 0), (0, block))),
        jnp.pad(both, ((0, 0), (0, 0), (block, 0))),
    )


def even_wide(x, block):
    groups, rows, width = x.shape
    if width % (2 * block) == 0:
        return x
    x = x.reshape(groups // 2, 2, rows, width)
    return jnp.transpose(x, (0, 2, 1, 3)).reshape(groups // 2, rows, 2 * width)


def on_device(
    coeffs_t,
    alpha_table,
    alpha_blocks,
    alpha_types,
    beta_table,
    beta_blocks,
    beta_types,
    row_counts,
):
    groups = lax.axis_size("col")
    rows = coeffs_t.shape[1]
    capacity = 3 * rows // (2 * groups)
    block = rows // alpha_blocks.shape[0]
    starts = (jnp.cumsum(row_counts) - row_counts).astype(jnp.int32)
    keep = lax.dynamic_slice(row_counts, (lax.axis_index("col"),), (1,))

    coeff_slots = slots_call(
        coeff_kernel, coeffs_t, starts, (), groups, capacity, ROW_PARTS, "coeff_slots"
    )
    own, partner = [], []
    for part in coeff_slots:
        got = lax.all_to_all(part, "col", split_axis=0, concat_axis=0, tiled=True)
        own.append(got)
        partner.append(swapped(got, "cls", 0))
    matrix = split_outside(alpha_matrix(alpha_table, alpha_blocks, alpha_types, block))
    (alpha_slots,) = slots_call(
        alpha_kernel, coeffs_t, starts, matrix, groups, capacity, 1, "alpha_slots"
    )
    alpha = lax.all_to_all(alpha_slots, "col", split_axis=0, concat_axis=0, tiled=True)
    left, right = beta_weights(beta_table, block)
    wide = lambda x: even_wide(x, block)
    return beta_call(
        [wide(x) for x in own],
        [wide(x) for x in partner],
        wide(alpha),
        left,
        right,
        beta_blocks.reshape(-1),
        beta_types.reshape(-1),
        keep,
        block,
    )


def solution(mesh):
    return jax.shard_map(
        on_device,
        mesh=mesh,
        in_specs=(P(("cls", "col"), None), P(), P(), P(), P(), P("cls", None), P("cls", None), P()),
        out_specs=P("col", "cls"),
        check_vma=False,
    )
```

```python
import functools

import jax
import jax.numpy as jnp
from jax import lax
from jax.experimental import pallas as pl
from jax.experimental.pallas import tpu as pltpu
from jax.sharding import PartitionSpec as P

ROW_PARTS = 3
TILE = 8
VMEM_BYTES = 56 * 1024 * 1024


def split_outside(x):
    high = lax.reduce_precision(x, 8, 7)
    return high.astype(jnp.bfloat16), (x - high).astype(jnp.bfloat16)


def split_inside(x):
    high = x.astype(jnp.bfloat16)
    return high, (x - high.astype(jnp.float32)).astype(jnp.bfloat16)


def column_chunk(width):
    for chunk in (512, 384, 256, 128):
        if width % chunk == 0:
            return chunk
    return width


def write_slots(starts, tall, out_refs):
    parts = len(out_refs)
    piece = out_refs[0].shape[1]
    for slot in range(out_refs[0].shape[0]):
        for part in range(parts):
            first = starts[slot] + part * piece
            shift = lax.rem(first, TILE)
            span = piece + TILE
            rows = pl.ds(pl.multiple_of(first - shift, TILE), span)
            moved = pltpu.roll(tall[rows, :], lax.rem(span - shift, span), 0)
            out_refs[part][slot] = moved[:piece]


def coeff_kernel(starts, coeffs, *rest):
    out_refs, tall = rest[:-1], rest[-1]
    rows = coeffs.shape[1]
    tall[:rows, :] = coeffs[...].T
    tall[rows:, :] = jnp.zeros((tall.shape[0] - rows, tall.shape[1]), jnp.float32)
    write_slots(starts, tall, out_refs)


def alpha_kernel(block, starts, types, coeffs, left, right, out_ref, tall, a_high, a_low):
    rows = coeffs.shape[1]
    count = rows // block

    @pl.when(pl.program_id(0) == 0)
    def _():
        def fill(at, carry):
            place = pl.ds(pl.multiple_of(at * block, block), block)
            for other in range(0, count, 2):
                first = types[at * count + other]
                second = types[at * count + other + 1]
                both = left[first] + right[second]
                a_high[place, other * block : (other + 2) * block] = both[:block]
                a_low[place, other * block : (other + 2) * block] = both[block:]
            return carry

        lax.fori_loop(0, count, fill, 0)

    c_high, c_low = split_inside(coeffs[...])
    dot = functools.partial(
        lax.dot_general,
        dimension_numbers=(((1,), (1,)), ((), ())),
        preferred_element_type=jnp.float32,
    )
    tall[:rows, :] = (dot(a_low[...], c_high) + dot(a_high[...], c_low)) + dot(
        a_high[...], c_high
    )
    tall[rows:, :] = jnp.zeros((tall.shape[0] - rows, tall.shape[1]), jnp.float32)
    write_slots(starts, tall, [out_ref])


def slots_call(kernel, coeffs_t, scalars, tables, scratch, groups, capacity, parts, name):
    width, rows = coeffs_t.shape
    chunk = column_chunk(width)
    piece = capacity // parts
    out = jax.ShapeDtypeStruct((groups, piece, width), jnp.float32)
    return pl.pallas_call(
        kernel,
        out_shape=[out] * parts,
        grid=(width // chunk,),
        in_specs=[pl.BlockSpec(memory_space=pltpu.SMEM)] * len(scalars)
        + [pl.BlockSpec((chunk, rows), lambda i: (i, 0))]
        + [pl.BlockSpec(table.shape, lambda i: (0, 0, 0)) for table in tables],
        out_specs=[pl.BlockSpec((groups, piece, chunk), lambda i: (0, 0, i))] * parts,
        scratch_shapes=[pltpu.VMEM((rows + capacity + TILE, chunk), jnp.float32), *scratch],
        compiler_params=pltpu.CompilerParams(vmem_limit_bytes=VMEM_BYTES),
        name=name,
    )(*scalars, coeffs_t, *tables)


def beta_kernel(steps, parts, block, keep, entries, types, *rest):
    own, partner = rest[:parts], rest[parts : 2 * parts]
    alpha, left, right, out, x_high, x_low = rest[2 * parts :]
    step = pl.program_id(0)
    width = alpha.shape[2]
    per_row = entries.shape[0] // (x_high.shape[0] // (2 * block))

    def store(pieces, at):
        tall = jnp.concatenate([piece[0] for piece in pieces], 0) if parts > 1 else pieces[0][0]
        high, low = split_inside(tall.T)
        rows = pl.ds(pl.multiple_of(at * width, block), width)
        x_high[rows, :] = high
        x_low[rows, :] = low

    @pl.when(step < steps)
    def _():
        store(own, step)

    @pl.when(jnp.logical_and(step >= steps, step < 2 * steps))
    def _():
        store(partner, step)

    def one(m):
        base = m * per_row
        places = [
            pl.ds(pl.multiple_of(entries[base + k] * block, block), block) for k in range(per_row)
        ]
        weights = jnp.concatenate(
            [
                left[types[base + k]] + right[types[base + k + 1]]
                for k in range(0, per_row, 2)
            ],
            1,
        )
        high = jnp.concatenate([x_high[place, :] for place in places], 0)
        low = jnp.concatenate([x_low[place, :] for place in places], 0)
        both = jnp.dot(weights, high, preferred_element_type=jnp.float32)
        cross = jnp.dot(weights[:block], low, preferred_element_type=jnp.float32)
        return both[:block] + (both[block:] + cross)

    @pl.when(step >= 2 * steps)
    def _():
        first = (step - 2 * steps) * (width // block)
        row = lax.broadcasted_iota(jnp.int32, (out.shape[0], 2 * block), 0)
        kept = row < keep[0]

        def pair(at, carry):
            m = first + 2 * at
            tall = jnp.concatenate([one(m), one(m + 1)], 0)
            lanes = pl.ds(pl.multiple_of(at * (2 * block), 2 * block), 2 * block)
            total = tall.T + alpha[0, :, lanes]
            out[:, lanes] = jnp.where(kept, total, jnp.float32(0.0))
            return carry

        lax.fori_loop(0, width // (2 * block), pair, 0)


def beta_call(own, partner, alpha, left, right, entries, types, keep, block):
    groups, capacity, width = alpha.shape
    parts = len(own)
    piece = capacity // parts
    whole = lambda a: pl.BlockSpec(a.shape, lambda i: (0, 0, 0))
    smem = pl.BlockSpec(memory_space=pltpu.SMEM)

    def at(offset):
        return lambda i: (jnp.clip(i - offset, 0, groups - 1), 0, 0)

    return pl.pallas_call(
        functools.partial(beta_kernel, groups, parts, block),
        out_shape=jax.ShapeDtypeStruct((capacity, groups * width), jnp.float32),
        grid=(3 * groups,),
        in_specs=[smem, smem, smem]
        + [pl.BlockSpec((1, piece, width), at(0))] * parts
        + [pl.BlockSpec((1, piece, width), at(groups))] * parts
        + [pl.BlockSpec((1, capacity, width), at(2 * groups)), whole(left), whole(right)],
        out_specs=pl.BlockSpec(
            (capacity, width), lambda i: (0, jnp.clip(i - 2 * groups, 0, groups - 1))
        ),
        scratch_shapes=[pltpu.VMEM((2 * groups * width, capacity), jnp.bfloat16)] * 2,
        compiler_params=pltpu.CompilerParams(vmem_limit_bytes=VMEM_BYTES),
        name="beta_sum",
    )(keep, entries, types, *own, *partner, alpha, left, right)


def exchange_kernel(groups, parts, *refs):
    own, alpha = refs[:parts], refs[parts]
    refs = refs[parts + 1 :]
    own_in, partner_in, alpha_in = refs[:parts], refs[parts : 2 * parts], refs[2 * parts]
    own_send, own_recv, far_send, far_recv, alpha_send, alpha_recv, local = refs[2 * parts + 1 :]
    cls, me = lax.axis_index("cls"), lax.axis_index("col")
    other = cls ^ 1

    barrier = pltpu.get_barrier_semaphore()
    for apart in range(1, groups):
        pl.semaphore_signal(
            barrier, inc=1, device_id=(cls, me ^ apart), device_id_type=pl.DeviceIdType.MESH
        )
    pl.semaphore_signal(
        barrier, inc=1, device_id=(other, me), device_id_type=pl.DeviceIdType.MESH
    )
    pl.semaphore_wait(barrier, groups)

    def near(source, target, apart, send, recv):
        return pltpu.make_async_remote_copy(
            src_ref=source.at[me ^ apart],
            dst_ref=target.at[me],
            send_sem=send,
            recv_sem=recv,
            device_id=(cls, me ^ apart),
            device_id_type=pl.DeviceIdType.MESH,
        )

    def far(part, apart):
        source = own[part] if apart == 0 else own_in[part]
        return pltpu.make_async_remote_copy(
            src_ref=source.at[me ^ apart],
            dst_ref=partner_in[part].at[me ^ apart],
            send_sem=far_send.at[part, apart],
            recv_sem=far_recv.at[part, apart],
            device_id=(other, me),
            device_id_type=pl.DeviceIdType.MESH,
        )

    aparts = range(1, groups)
    own_copies = [
        [near(own[p], own_in[p], x, own_send.at[p, x], own_recv.at[p, x]) for x in aparts]
        for p in range(parts)
    ]
    alpha_copies = [near(alpha, alpha_in, x, alpha_send.at[x], alpha_recv.at[x]) for x in aparts]
    far_copies = [[far(p, x) for x in range(groups)] for p in range(parts)]
    local_copies = [
        pltpu.make_async_copy(own[p].at[me], own_in[p].at[me], local.at[p]) for p in range(parts)
    ] + [pltpu.make_async_copy(alpha.at[me], alpha_in.at[me], local.at[parts])]
    waves = own_copies + [alpha_copies]

    for part in range(parts):
        far_copies[part][0].start()
    for copy in waves[0] + waves[1]:
        copy.start()
    for copy in local_copies:
        copy.start()
    for part in range(parts):
        for at, copy in enumerate(own_copies[part]):
            copy.wait_recv()
            far_copies[part][at + 1].start()
        if part + 2 < len(waves):
            for copy in waves[part + 2]:
                copy.start()
    for copy in alpha_copies:
        copy.wait_recv()
    for copies in far_copies:
        for copy in copies:
            copy.wait_recv()
    for copy in local_copies:
        copy.wait()
    for copies in waves + far_copies:
        for copy in copies:
            copy.wait_send()


def exchange_call(own, alpha):
    groups = alpha.shape[0]
    parts = len(own)
    shape = lambda x: jax.ShapeDtypeStruct(x.shape, x.dtype)
    outs = [shape(x) for x in own] * 2 + [shape(alpha)]
    dma = pltpu.SemaphoreType.DMA
    got = pl.pallas_call(
        functools.partial(exchange_kernel, groups, parts),
        out_shape=outs,
        in_specs=[pl.BlockSpec(memory_space=pl.ANY)] * (parts + 1),
        out_specs=[pl.BlockSpec(memory_space=pl.ANY)] * len(outs),
        scratch_shapes=[dma((parts, groups))] * 4 + [dma((groups,))] * 2 + [dma((parts + 1,))],
        compiler_params=pltpu.CompilerParams(
            collective_id=0, has_side_effects=True, vmem_limit_bytes=VMEM_BYTES
        ),
        name="exchange",
    )(*own, alpha)
    return got[:parts], got[parts : 2 * parts], got[2 * parts]


def alpha_entries(alpha_blocks, alpha_types, missing):
    count = alpha_blocks.shape[0]
    hit = alpha_blocks[:, :, None] == jnp.arange(count, dtype=jnp.int32)[None, None, :]
    type_of = jnp.sum(jnp.where(hit, alpha_types[:, :, None], 0), 1)
    return jnp.where(jnp.any(hit, 1), type_of, missing).reshape(-1).astype(jnp.int32)


def weights(tables):
    block = tables.shape[2]
    both = jnp.concatenate(split_outside(tables), 1)
    return (
        jnp.pad(both, ((0, 0), (0, 0), (0, block))),
        jnp.pad(both, ((0, 0), (0, 0), (block, 0))),
    )


def alpha_weights(alpha_table, block):
    tables = alpha_table.reshape(-1, block, block)
    return weights(jnp.pad(tables, ((0, 1), (0, 0), (0, 0))))


def beta_weights(beta_table, block):
    return weights(jnp.transpose(beta_table.reshape(-1, block, block), (0, 2, 1)))


def alpha_call(coeffs_t, starts, alpha_table, alpha_blocks, alpha_types, groups, capacity, block):
    rows = coeffs_t.shape[1]
    types = alpha_entries(alpha_blocks, alpha_types, alpha_table.shape[0])
    return slots_call(
        functools.partial(alpha_kernel, block),
        coeffs_t,
        (starts, types),
        alpha_weights(alpha_table, block),
        [pltpu.VMEM((rows, rows), jnp.bfloat16)] * 2,
        groups,
        capacity,
        1,
        "alpha_slots",
    )[0]


def even_wide(x, block):
    groups, rows, width = x.shape
    if width % (2 * block) == 0:
        return x
    x = x.reshape(groups // 2, 2, rows, width)
    return jnp.transpose(x, (0, 2, 1, 3)).reshape(groups // 2, rows, 2 * width)


def on_device(
    coeffs_t,
    alpha_table,
    alpha_blocks,
    alpha_types,
    beta_table,
    beta_blocks,
    beta_types,
    row_counts,
):
    groups = lax.axis_size("col")
    rows = coeffs_t.shape[1]
    capacity = 3 * rows // (2 * groups)
    block = rows // alpha_blocks.shape[0]
    starts = (jnp.cumsum(row_counts) - row_counts).astype(jnp.int32)
    keep = lax.dynamic_slice(row_counts, (lax.axis_index("col"),), (1,))

    coeff_slots = slots_call(
        coeff_kernel, coeffs_t, (starts,), (), (), groups, capacity, ROW_PARTS, "coeff_slots"
    )
    alpha_slots = alpha_call(
        coeffs_t, starts, alpha_table, alpha_blocks, alpha_types, groups, capacity, block
    )
    own, partner, alpha = exchange_call(coeff_slots, alpha_slots)
    left, right = beta_weights(beta_table, block)
    wide = lambda x: even_wide(x, block)
    return beta_call(
        [wide(x) for x in own],
        [wide(x) for x in partner],
        wide(alpha),
        left,
        right,
        beta_blocks.reshape(-1),
        beta_types.reshape(-1),
        keep,
        block,
    )


def solution(mesh):
    return jax.shard_map(
        on_device,
        mesh=mesh,
        in_specs=(P(("cls", "col"), None), P(), P(), P(), P(), P("cls", None), P("cls", None), P()),
        out_specs=P("col", "cls"),
        check_vma=False,
    )
```

```python
import functools

import jax
import jax.numpy as jnp
from jax import lax
from jax.experimental import pallas as pl
from jax.experimental.pallas import tpu as pltpu
from jax.sharding import PartitionSpec as P

ROW_PARTS = 3
TILE = 8
VMEM_BYTES = 56 * 1024 * 1024


def split_outside(x):
    high = lax.reduce_precision(x, 8, 7)
    return high.astype(jnp.bfloat16), (x - high).astype(jnp.bfloat16)


def split_inside(x):
    high = x.astype(jnp.bfloat16)
    return high, (x - high.astype(jnp.float32)).astype(jnp.bfloat16)


def column_chunk(width):
    for chunk in (512, 384, 256, 128):
        if width % chunk == 0:
            return chunk
    return width


def write_slots(starts, tall, out_refs):
    parts = len(out_refs)
    piece = out_refs[0].shape[1]
    for slot in range(out_refs[0].shape[0]):
        for part in range(parts):
            first = starts[slot] + part * piece
            shift = lax.rem(first, TILE)
            span = piece + TILE
            rows = pl.ds(pl.multiple_of(first - shift, TILE), span)
            moved = pltpu.roll(tall[rows, :], lax.rem(span - shift, span), 0)
            out_refs[part][slot] = moved[:piece]


def coeff_kernel(starts, coeffs, *rest):
    out_refs, tall = rest[:-1], rest[-1]
    rows = coeffs.shape[1]
    tall[:rows, :] = coeffs[...].T
    tall[rows:, :] = jnp.zeros((tall.shape[0] - rows, tall.shape[1]), jnp.float32)
    write_slots(starts, tall, out_refs)


def alpha_rows_kernel(block, starts, types, left, right, high_ref, low_ref, tall):
    rows = tall.shape[1]
    count = rows // block
    groups, capacity = high_ref.shape[:2]

    def fill(at, carry):
        place = pl.ds(pl.multiple_of(at * block, block), block)
        for other in range(0, count, 2):
            first = types[at * count + other]
            second = types[at * count + other + 1]
            tall[place, other * block : (other + 2) * block] = left[first] + right[second]
        return carry

    lax.fori_loop(0, count, fill, 0)
    tall[rows:, :] = jnp.zeros((tall.shape[0] - rows, rows), jnp.float32)
    for slot in range(groups):
        shift = lax.rem(starts[slot], TILE)
        span = capacity + TILE
        place = pl.ds(pl.multiple_of(starts[slot] - shift, TILE), span)
        moved = pltpu.roll(tall[place, :], lax.rem(span - shift, span), 0)
        high_ref[slot], low_ref[slot] = split_inside(moved[:capacity])


def alpha_rows_call(starts, types, left, right, rows, groups, capacity, block):
    out = jax.ShapeDtypeStruct((groups, capacity, rows), jnp.bfloat16)
    return pl.pallas_call(
        functools.partial(alpha_rows_kernel, block),
        out_shape=[out] * 2,
        in_specs=[pl.BlockSpec(memory_space=pltpu.SMEM)] * 2
        + [pl.BlockSpec(memory_space=pltpu.VMEM)] * 2,
        out_specs=[pl.BlockSpec(memory_space=pltpu.VMEM)] * 2,
        scratch_shapes=[pltpu.VMEM((rows + capacity + TILE, rows), jnp.float32)],
        compiler_params=pltpu.CompilerParams(vmem_limit_bytes=VMEM_BYTES),
        name="alpha_rows",
    )(starts, types, left, right)


def alpha_product(chunk, coeffs, a_high, a_low, out):
    dot = functools.partial(
        lax.dot_general,
        dimension_numbers=(((1,), (1,)), ((), ())),
        preferred_element_type=jnp.float32,
    )
    for first in range(0, coeffs.shape[0], chunk):
        c_high, c_low = split_inside(coeffs[first : first + chunk, :])
        for slot in range(out.shape[0]):
            total = (dot(a_low[slot], c_high) + dot(a_high[slot], c_low)) + dot(
                a_high[slot], c_high
            )
            out[slot, :, first : first + chunk] = total


def slots_call(coeffs_t, starts, groups, capacity, parts):
    width, rows = coeffs_t.shape
    chunk = column_chunk(width)
    piece = capacity // parts
    out = jax.ShapeDtypeStruct((groups, piece, width), jnp.float32)
    return pl.pallas_call(
        coeff_kernel,
        out_shape=[out] * parts,
        grid=(width // chunk,),
        in_specs=[
            pl.BlockSpec(memory_space=pltpu.SMEM),
            pl.BlockSpec((chunk, rows), lambda i: (i, 0)),
        ],
        out_specs=[pl.BlockSpec((groups, piece, chunk), lambda i: (0, 0, i))] * parts,
        scratch_shapes=[pltpu.VMEM((rows + capacity + TILE, chunk), jnp.float32)],
        compiler_params=pltpu.CompilerParams(vmem_limit_bytes=VMEM_BYTES),
        name="coeff_slots",
    )(starts, coeffs_t)


def beta_kernel(steps, parts, block, keep, entries, types, *rest):
    own, partner = rest[:parts], rest[parts : 2 * parts]
    alpha, left, right, out, x_high, x_low = rest[2 * parts :]
    step = pl.program_id(0)
    width = alpha.shape[2]
    per_row = entries.shape[0] // (x_high.shape[0] // (2 * block))

    def store(pieces, at):
        tall = jnp.concatenate([piece[0] for piece in pieces], 0) if parts > 1 else pieces[0][0]
        high, low = split_inside(tall.T)
        rows = pl.ds(pl.multiple_of(at * width, block), width)
        x_high[rows, :] = high
        x_low[rows, :] = low

    @pl.when(step < steps)
    def _():
        store(own, step)

    @pl.when(jnp.logical_and(step >= steps, step < 2 * steps))
    def _():
        store(partner, step)

    def one(m):
        base = m * per_row
        places = [
            pl.ds(pl.multiple_of(entries[base + k] * block, block), block) for k in range(per_row)
        ]
        weights = jnp.concatenate(
            [
                left[types[base + k]] + right[types[base + k + 1]]
                for k in range(0, per_row, 2)
            ],
            1,
        )
        high = jnp.concatenate([x_high[place, :] for place in places], 0)
        low = jnp.concatenate([x_low[place, :] for place in places], 0)
        both = jnp.dot(weights, high, preferred_element_type=jnp.float32)
        cross = jnp.dot(weights[:block], low, preferred_element_type=jnp.float32)
        return both[:block] + (both[block:] + cross)

    @pl.when(step >= 2 * steps)
    def _():
        first = (step - 2 * steps) * (width // block)
        row = lax.broadcasted_iota(jnp.int32, (out.shape[0], 2 * block), 0)
        kept = row < keep[0]

        pairs = width // (2 * block)
        together = 4 if pairs % 4 == 0 else 1

        def some_pairs(turn, carry):
            for nth in range(together):
                at = turn * together + nth
                m = first + 2 * at
                tall = jnp.concatenate([one(m), one(m + 1)], 0)
                lanes = pl.ds(pl.multiple_of(at * (2 * block), 2 * block), 2 * block)
                total = tall.T + alpha[0, :, lanes]
                out[:, lanes] = jnp.where(kept, total, jnp.float32(0.0))
            return carry

        lax.fori_loop(0, pairs // together, some_pairs, 0)


def beta_call(own, partner, alpha, left, right, entries, types, keep, block):
    groups, capacity, width = alpha.shape
    parts = len(own)
    piece = capacity // parts
    whole = lambda a: pl.BlockSpec(a.shape, lambda i: (0, 0, 0))
    smem = pl.BlockSpec(memory_space=pltpu.SMEM)

    def at(offset):
        return lambda i: (jnp.clip(i - offset, 0, groups - 1), 0, 0)

    return pl.pallas_call(
        functools.partial(beta_kernel, groups, parts, block),
        out_shape=jax.ShapeDtypeStruct((capacity, groups * width), jnp.float32),
        grid=(3 * groups,),
        in_specs=[smem, smem, smem]
        + [pl.BlockSpec((1, piece, width), at(0))] * parts
        + [pl.BlockSpec((1, piece, width), at(groups))] * parts
        + [pl.BlockSpec((1, capacity, width), at(2 * groups)), whole(left), whole(right)],
        out_specs=pl.BlockSpec(
            (capacity, width), lambda i: (0, jnp.clip(i - 2 * groups, 0, groups - 1))
        ),
        scratch_shapes=[pltpu.VMEM((2 * groups * width, capacity), jnp.bfloat16)] * 2,
        compiler_params=pltpu.CompilerParams(vmem_limit_bytes=VMEM_BYTES),
        name="beta_sum",
    )(keep, entries, types, *own, *partner, alpha, left, right)


def exchange_kernel(groups, parts, chunk, a_high, a_low, coeffs, *refs):
    own = refs[:parts]
    refs = refs[parts:]
    own_in, partner_in, alpha_in = refs[:parts], refs[parts : 2 * parts], refs[2 * parts]
    own_send, own_recv, far_send, far_recv, alpha_send, alpha_recv, local = refs[
        2 * parts + 1 : 2 * parts + 8
    ]
    held, alpha, held_high, held_low = refs[2 * parts + 8 :]
    cls, me = lax.axis_index("cls"), lax.axis_index("col")
    other = cls ^ 1

    barrier = pltpu.get_barrier_semaphore()
    for apart in range(1, groups):
        pl.semaphore_signal(
            barrier, inc=1, device_id=(cls, me ^ apart), device_id_type=pl.DeviceIdType.MESH
        )
    pl.semaphore_signal(
        barrier, inc=1, device_id=(other, me), device_id_type=pl.DeviceIdType.MESH
    )
    pl.semaphore_wait(barrier, groups)

    def near(source, target, apart, send, recv):
        return pltpu.make_async_remote_copy(
            src_ref=source.at[me ^ apart],
            dst_ref=target.at[me],
            send_sem=send,
            recv_sem=recv,
            device_id=(cls, me ^ apart),
            device_id_type=pl.DeviceIdType.MESH,
        )

    def far(part, apart):
        source = own[part] if apart == 0 else own_in[part]
        return pltpu.make_async_remote_copy(
            src_ref=source.at[me ^ apart],
            dst_ref=partner_in[part].at[me ^ apart],
            send_sem=far_send.at[part, apart],
            recv_sem=far_recv.at[part, apart],
            device_id=(other, me),
            device_id_type=pl.DeviceIdType.MESH,
        )

    aparts = range(1, groups)
    own_copies = [
        [near(own[p], own_in[p], x, own_send.at[p, x], own_recv.at[p, x]) for x in aparts]
        for p in range(parts)
    ]
    alpha_copies = [near(alpha, alpha_in, x, alpha_send.at[x], alpha_recv.at[x]) for x in aparts]
    far_copies = [[far(p, x) for x in range(groups)] for p in range(parts)]
    local_copies = [
        pltpu.make_async_copy(own[p].at[me], own_in[p].at[me], local.at[p]) for p in range(parts)
    ]
    alpha_local = pltpu.make_async_copy(alpha.at[me], alpha_in.at[me], local.at[parts])
    loading = [
        pltpu.make_async_copy(source, target, local.at[parts + 1 + nth])
        for nth, (source, target) in enumerate(
            [(coeffs, held), (a_high, held_high), (a_low, held_low)]
        )
    ]
    waves = own_copies + [alpha_copies]

    for copy in loading:
        copy.start()
    for part in range(parts):
        far_copies[part][0].start()
    for copy in waves[0] + waves[1]:
        copy.start()
    for copy in local_copies:
        copy.start()
    for copy in loading:
        copy.wait()
    alpha_product(chunk, held, held_high, held_low, alpha)
    alpha_local.start()
    for part in range(parts):
        for at, copy in enumerate(own_copies[part]):
            copy.wait_recv()
            far_copies[part][at + 1].start()
        if part + 2 < len(waves):
            for copy in waves[part + 2]:
                copy.start()
    for copy in alpha_copies:
        copy.wait_recv()
    for copies in far_copies:
        for copy in copies:
            copy.wait_recv()
    for copy in local_copies + [alpha_local]:
        copy.wait()
    for copies in waves + far_copies:
        for copy in copies:
            copy.wait_send()


def exchange_call(own, coeffs_t, a_high, a_low):
    groups, piece, width = own[0].shape
    parts = len(own)
    capacity = parts * piece
    shape = lambda x: jax.ShapeDtypeStruct(x.shape, x.dtype)
    alpha = jax.ShapeDtypeStruct((groups, capacity, width), jnp.float32)
    outs = [shape(x) for x in own] * 2 + [alpha]
    dma = pltpu.SemaphoreType.DMA
    anywhere = pl.BlockSpec(memory_space=pl.ANY)
    got = pl.pallas_call(
        functools.partial(exchange_kernel, groups, parts, column_chunk(width)),
        out_shape=outs,
        in_specs=[anywhere] * (parts + 3),
        out_specs=[anywhere] * len(outs),
        scratch_shapes=[dma((parts, groups))] * 4
        + [dma((groups,))] * 2
        + [dma((parts + 4,))]
        + [
            pltpu.VMEM(coeffs_t.shape, jnp.float32),
            pltpu.VMEM(alpha.shape, jnp.float32),
            pltpu.VMEM(a_high.shape, jnp.bfloat16),
            pltpu.VMEM(a_low.shape, jnp.bfloat16),
        ],
        compiler_params=pltpu.CompilerParams(
            collective_id=0, has_side_effects=True, vmem_limit_bytes=VMEM_BYTES
        ),
        name="exchange",
    )(a_high, a_low, coeffs_t, *own)
    return got[:parts], got[parts : 2 * parts], got[2 * parts]


def alpha_entries(alpha_blocks, alpha_types, missing):
    count = alpha_blocks.shape[0]
    hit = alpha_blocks[:, :, None] == jnp.arange(count, dtype=jnp.int32)[None, None, :]
    type_of = jnp.sum(jnp.where(hit, alpha_types[:, :, None], 0), 1)
    return jnp.where(jnp.any(hit, 1), type_of, missing).reshape(-1).astype(jnp.int32)


def weights(tables):
    block = tables.shape[2]
    both = jnp.concatenate(split_outside(tables), 1)
    return (
        jnp.pad(both, ((0, 0), (0, 0), (0, block))),
        jnp.pad(both, ((0, 0), (0, 0), (block, 0))),
    )


def alpha_weights(alpha_table, block):
    tables = jnp.pad(alpha_table.reshape(-1, block, block), ((0, 1), (0, 0), (0, 0)))
    return (
        jnp.pad(tables, ((0, 0), (0, 0), (0, block))),
        jnp.pad(tables, ((0, 0), (0, 0), (block, 0))),
    )


def beta_weights(beta_table, block):
    return weights(jnp.transpose(beta_table.reshape(-1, block, block), (0, 2, 1)))


def even_wide(x, block):
    groups, rows, width = x.shape
    if width % (2 * block) == 0:
        return x
    x = x.reshape(groups // 2, 2, rows, width)
    return jnp.transpose(x, (0, 2, 1, 3)).reshape(groups // 2, rows, 2 * width)


def on_device(
    coeffs_t,
    alpha_table,
    alpha_blocks,
    alpha_types,
    beta_table,
    beta_blocks,
    beta_types,
    row_counts,
):
    groups = lax.axis_size("col")
    rows = coeffs_t.shape[1]
    capacity = 3 * rows // (2 * groups)
    block = rows // alpha_blocks.shape[0]
    starts = (jnp.cumsum(row_counts) - row_counts).astype(jnp.int32)
    keep = lax.dynamic_slice(row_counts, (lax.axis_index("col"),), (1,))

    coeff_slots = slots_call(coeffs_t, starts, groups, capacity, ROW_PARTS)
    types = alpha_entries(alpha_blocks, alpha_types, alpha_table.shape[0])
    a_high, a_low = alpha_rows_call(
        starts, types, *alpha_weights(alpha_table, block), rows, groups, capacity, block
    )
    own, partner, alpha = exchange_call(coeff_slots, coeffs_t, a_high, a_low)
    left, right = beta_weights(beta_table, block)
    wide = lambda x: even_wide(x, block)
    return beta_call(
        [wide(x) for x in own],
        [wide(x) for x in partner],
        wide(alpha),
        left,
        right,
        beta_blocks.reshape(-1),
        beta_types.reshape(-1),
        keep,
        block,
    )


def solution(mesh):
    return jax.shard_map(
        on_device,
        mesh=mesh,
        in_specs=(P(("cls", "col"), None), P(), P(), P(), P(), P("cls", None), P("cls", None), P()),
        out_specs=P("col", "cls"),
        check_vma=False,
    )
```

```python
import functools

import jax
import jax.numpy as jnp
from jax import lax
from jax.experimental import pallas as pl
from jax.experimental.pallas import tpu as pltpu
from jax.sharding import PartitionSpec as P

ROW_PARTS = 3
TILE = 8
VMEM_BYTES = 56 * 1024 * 1024


def split_outside(x):
    high = lax.reduce_precision(x, 8, 7)
    return high.astype(jnp.bfloat16), (x - high).astype(jnp.bfloat16)


def split_inside(x):
    high = x.astype(jnp.bfloat16)
    return high, (x - high.astype(jnp.float32)).astype(jnp.bfloat16)


def column_chunk(width):
    for chunk in (512, 384, 256, 128):
        if width % chunk == 0:
            return chunk
    return width


def write_slots(starts, tall, out_refs):
    parts = len(out_refs)
    piece = out_refs[0].shape[1]
    for slot in range(out_refs[0].shape[0]):
        for part in range(parts):
            first = starts[slot] + part * piece
            shift = lax.rem(first, TILE)
            span = piece + TILE
            rows = pl.ds(pl.multiple_of(first - shift, TILE), span)
            moved = pltpu.roll(tall[rows, :], lax.rem(span - shift, span), 0)
            out_refs[part][slot] = moved[:piece]


def coeff_kernel(starts, coeffs, *rest):
    out_refs, tall = rest[:-1], rest[-1]
    rows = coeffs.shape[1]
    tall[:rows, :] = coeffs[...].T
    tall[rows:, :] = jnp.zeros((tall.shape[0] - rows, tall.shape[1]), jnp.float32)
    write_slots(starts, tall, out_refs)


def alpha_rows_kernel(block, starts, types, left, right, high_ref, low_ref, tall):
    rows = tall.shape[1]
    count = rows // block
    groups, capacity = high_ref.shape[:2]

    def fill(at, carry):
        place = pl.ds(pl.multiple_of(at * block, block), block)
        for other in range(0, count, 2):
            first = types[at * count + other]
            second = types[at * count + other + 1]
            tall[place, other * block : (other + 2) * block] = left[first] + right[second]
        return carry

    lax.fori_loop(0, count, fill, 0)
    tall[rows:, :] = jnp.zeros((tall.shape[0] - rows, rows), jnp.float32)
    for slot in range(groups):
        shift = lax.rem(starts[slot], TILE)
        span = capacity + TILE
        place = pl.ds(pl.multiple_of(starts[slot] - shift, TILE), span)
        moved = pltpu.roll(tall[place, :], lax.rem(span - shift, span), 0)
        high_ref[slot], low_ref[slot] = split_inside(moved[:capacity])


def alpha_rows_call(starts, types, left, right, rows, groups, capacity, block):
    out = jax.ShapeDtypeStruct((groups, capacity, rows), jnp.bfloat16)
    return pl.pallas_call(
        functools.partial(alpha_rows_kernel, block),
        out_shape=[out] * 2,
        in_specs=[pl.BlockSpec(memory_space=pltpu.SMEM)] * 2
        + [pl.BlockSpec(memory_space=pltpu.VMEM)] * 2,
        out_specs=[pl.BlockSpec(memory_space=pltpu.VMEM)] * 2,
        scratch_shapes=[pltpu.VMEM((rows + capacity + TILE, rows), jnp.float32)],
        compiler_params=pltpu.CompilerParams(vmem_limit_bytes=VMEM_BYTES),
        name="alpha_rows",
    )(starts, types, left, right)


def alpha_product(chunk, coeffs, a_high, a_low, out):
    dot = functools.partial(
        lax.dot_general,
        dimension_numbers=(((1,), (1,)), ((), ())),
        preferred_element_type=jnp.float32,
    )
    for first in range(0, coeffs.shape[0], chunk):
        c_high, c_low = split_inside(coeffs[first : first + chunk, :])
        for slot in range(out.shape[0]):
            total = (dot(a_low[slot], c_high) + dot(a_high[slot], c_low)) + dot(
                a_high[slot], c_high
            )
            out[slot, :, first : first + chunk] = total


def slots_call(coeffs_t, starts, groups, capacity, parts):
    width, rows = coeffs_t.shape
    chunk = column_chunk(width)
    piece = capacity // parts
    out = jax.ShapeDtypeStruct((groups, piece, width), jnp.float32)
    return pl.pallas_call(
        coeff_kernel,
        out_shape=[out] * parts,
        grid=(width // chunk,),
        in_specs=[
            pl.BlockSpec(memory_space=pltpu.SMEM),
            pl.BlockSpec((chunk, rows), lambda i: (i, 0)),
        ],
        out_specs=[pl.BlockSpec((groups, piece, chunk), lambda i: (0, 0, i))] * parts,
        scratch_shapes=[pltpu.VMEM((rows + capacity + TILE, chunk), jnp.float32)],
        compiler_params=pltpu.CompilerParams(vmem_limit_bytes=VMEM_BYTES),
        name="coeff_slots",
    )(starts, coeffs_t)


def beta_kernel(steps, parts, block, keep, entries, types, *rest):
    own, partner = rest[:parts], rest[parts : 2 * parts]
    alpha, left, right, out, x_high, x_low = rest[2 * parts :]
    step = pl.program_id(0)
    width = alpha.shape[2]
    per_row = entries.shape[0] // (x_high.shape[0] // (2 * block))

    def store(pieces, at):
        tall = jnp.concatenate([piece[0] for piece in pieces], 0) if parts > 1 else pieces[0][0]
        high, low = split_inside(tall.T)
        rows = pl.ds(pl.multiple_of(at * width, block), width)
        x_high[rows, :] = high
        x_low[rows, :] = low

    @pl.when(step < steps)
    def _():
        store(own, step)

    @pl.when(jnp.logical_and(step >= steps, step < 2 * steps))
    def _():
        store(partner, step)

    def one(m):
        base = m * per_row
        places = [
            pl.ds(pl.multiple_of(entries[base + k] * block, block), block) for k in range(per_row)
        ]
        weights = jnp.concatenate(
            [
                left[types[base + k]] + right[types[base + k + 1]]
                for k in range(0, per_row, 2)
            ],
            1,
        )
        high = jnp.concatenate([x_high[place, :] for place in places], 0)
        low = jnp.concatenate([x_low[place, :] for place in places], 0)
        both = jnp.dot(weights, high, preferred_element_type=jnp.float32)
        cross = jnp.dot(weights[:block], low, preferred_element_type=jnp.float32)
        return both[:block] + (both[block:] + cross)

    @pl.when(step >= 2 * steps)
    def _():
        first = (step - 2 * steps) * (width // block)
        row = lax.broadcasted_iota(jnp.int32, (out.shape[0], 2 * block), 0)
        kept = row < keep[0]

        pairs = width // (2 * block)
        together = next(n for n in (12, 6, 4, 3, 2, 1) if pairs % n == 0)

        def some_pairs(turn, carry):
            for nth in range(together):
                at = turn * together + nth
                m = first + 2 * at
                tall = jnp.concatenate([one(m), one(m + 1)], 0)
                lanes = pl.ds(pl.multiple_of(at * (2 * block), 2 * block), 2 * block)
                total = tall.T + alpha[0, :, lanes]
                out[:, lanes] = jnp.where(kept, total, jnp.float32(0.0))
            return carry

        lax.fori_loop(0, pairs // together, some_pairs, 0)


def beta_call(own, partner, alpha, left, right, entries, types, keep, block):
    groups, capacity, width = alpha.shape
    parts = len(own)
    piece = capacity // parts
    whole = lambda a: pl.BlockSpec(a.shape, lambda i: (0, 0, 0))
    smem = pl.BlockSpec(memory_space=pltpu.SMEM)

    def at(offset):
        return lambda i: (jnp.clip(i - offset, 0, groups - 1), 0, 0)

    return pl.pallas_call(
        functools.partial(beta_kernel, groups, parts, block),
        out_shape=jax.ShapeDtypeStruct((capacity, groups * width), jnp.float32),
        grid=(3 * groups,),
        in_specs=[smem, smem, smem]
        + [pl.BlockSpec((1, piece, width), at(0))] * parts
        + [pl.BlockSpec((1, piece, width), at(groups))] * parts
        + [pl.BlockSpec((1, capacity, width), at(2 * groups)), whole(left), whole(right)],
        out_specs=pl.BlockSpec(
            (capacity, width), lambda i: (0, jnp.clip(i - 2 * groups, 0, groups - 1))
        ),
        scratch_shapes=[pltpu.VMEM((2 * groups * width, capacity), jnp.bfloat16)] * 2,
        compiler_params=pltpu.CompilerParams(vmem_limit_bytes=VMEM_BYTES),
        name="beta_sum",
    )(keep, entries, types, *own, *partner, alpha, left, right)


def exchange_kernel(groups, parts, chunk, a_high, a_low, coeffs, *refs):
    own = refs[:parts]
    refs = refs[parts:]
    own_in, partner_in, alpha_in = refs[:parts], refs[parts : 2 * parts], refs[2 * parts]
    own_send, own_recv, far_send, far_recv, alpha_send, alpha_recv, local = refs[
        2 * parts + 1 : 2 * parts + 8
    ]
    held, alpha, held_high, held_low = refs[2 * parts + 8 :]
    cls, me = lax.axis_index("cls"), lax.axis_index("col")
    other = cls ^ 1

    barrier = pltpu.get_barrier_semaphore()
    for apart in range(1, groups):
        pl.semaphore_signal(
            barrier, inc=1, device_id=(cls, me ^ apart), device_id_type=pl.DeviceIdType.MESH
        )
    pl.semaphore_signal(
        barrier, inc=1, device_id=(other, me), device_id_type=pl.DeviceIdType.MESH
    )
    pl.semaphore_wait(barrier, groups)

    def near(source, target, apart, send, recv):
        return pltpu.make_async_remote_copy(
            src_ref=source.at[me ^ apart],
            dst_ref=target.at[me],
            send_sem=send,
            recv_sem=recv,
            device_id=(cls, me ^ apart),
            device_id_type=pl.DeviceIdType.MESH,
        )

    def far(part, apart):
        source = own[part] if apart == 0 else own_in[part]
        return pltpu.make_async_remote_copy(
            src_ref=source.at[me ^ apart],
            dst_ref=partner_in[part].at[me ^ apart],
            send_sem=far_send.at[part, apart],
            recv_sem=far_recv.at[part, apart],
            device_id=(other, me),
            device_id_type=pl.DeviceIdType.MESH,
        )

    aparts = range(1, groups)
    own_copies = [
        [near(own[p], own_in[p], x, own_send.at[p, x], own_recv.at[p, x]) for x in aparts]
        for p in range(parts)
    ]
    alpha_copies = [near(alpha, alpha_in, x, alpha_send.at[x], alpha_recv.at[x]) for x in aparts]
    far_copies = [[far(p, x) for x in range(groups)] for p in range(parts)]
    local_copies = [
        pltpu.make_async_copy(own[p].at[me], own_in[p].at[me], local.at[p]) for p in range(parts)
    ]
    alpha_local = pltpu.make_async_copy(alpha.at[me], alpha_in.at[me], local.at[parts])
    loading = [
        pltpu.make_async_copy(source, target, local.at[parts + 1 + nth])
        for nth, (source, target) in enumerate(
            [(coeffs, held), (a_high, held_high), (a_low, held_low)]
        )
    ]
    waves = own_copies + [alpha_copies]

    for copy in loading:
        copy.start()
    for part in range(parts):
        far_copies[part][0].start()
    for copy in waves[0] + waves[1]:
        copy.start()
    for copy in local_copies:
        copy.start()
    for copy in loading:
        copy.wait()
    alpha_product(chunk, held, held_high, held_low, alpha)
    alpha_local.start()
    for part in range(parts):
        for at, copy in enumerate(own_copies[part]):
            copy.wait_recv()
            far_copies[part][at + 1].start()
        if part + 2 < len(waves):
            for copy in waves[part + 2]:
                copy.start()
    for copy in alpha_copies:
        copy.wait_recv()
    for copies in far_copies:
        for copy in copies:
            copy.wait_recv()
    for copy in local_copies + [alpha_local]:
        copy.wait()
    for copies in waves + far_copies:
        for copy in copies:
            copy.wait_send()


def exchange_call(own, coeffs_t, a_high, a_low):
    groups, piece, width = own[0].shape
    parts = len(own)
    capacity = parts * piece
    shape = lambda x: jax.ShapeDtypeStruct(x.shape, x.dtype)
    alpha = jax.ShapeDtypeStruct((groups, capacity, width), jnp.float32)
    outs = [shape(x) for x in own] * 2 + [alpha]
    dma = pltpu.SemaphoreType.DMA
    anywhere = pl.BlockSpec(memory_space=pl.ANY)
    got = pl.pallas_call(
        functools.partial(exchange_kernel, groups, parts, column_chunk(width)),
        out_shape=outs,
        in_specs=[anywhere] * (parts + 3),
        out_specs=[anywhere] * len(outs),
        scratch_shapes=[dma((parts, groups))] * 4
        + [dma((groups,))] * 2
        + [dma((parts + 4,))]
        + [
            pltpu.VMEM(coeffs_t.shape, jnp.float32),
            pltpu.VMEM(alpha.shape, jnp.float32),
            pltpu.VMEM(a_high.shape, jnp.bfloat16),
            pltpu.VMEM(a_low.shape, jnp.bfloat16),
        ],
        compiler_params=pltpu.CompilerParams(
            collective_id=0, has_side_effects=True, vmem_limit_bytes=VMEM_BYTES
        ),
        name="exchange",
    )(a_high, a_low, coeffs_t, *own)
    return got[:parts], got[parts : 2 * parts], got[2 * parts]


def alpha_entries(alpha_blocks, alpha_types, missing):
    count = alpha_blocks.shape[0]
    hit = alpha_blocks[:, :, None] == jnp.arange(count, dtype=jnp.int32)[None, None, :]
    type_of = jnp.sum(jnp.where(hit, alpha_types[:, :, None], 0), 1)
    return jnp.where(jnp.any(hit, 1), type_of, missing).reshape(-1).astype(jnp.int32)


def weights(tables):
    block = tables.shape[2]
    both = jnp.concatenate(split_outside(tables), 1)
    return (
        jnp.pad(both, ((0, 0), (0, 0), (0, block))),
        jnp.pad(both, ((0, 0), (0, 0), (block, 0))),
    )


def alpha_weights(alpha_table, block):
    tables = jnp.pad(alpha_table.reshape(-1, block, block), ((0, 1), (0, 0), (0, 0)))
    return (
        jnp.pad(tables, ((0, 0), (0, 0), (0, block))),
        jnp.pad(tables, ((0, 0), (0, 0), (block, 0))),
    )


def beta_weights(beta_table, block):
    return weights(jnp.transpose(beta_table.reshape(-1, block, block), (0, 2, 1)))


def even_wide(x, block):
    groups, rows, width = x.shape
    if width % (2 * block) == 0:
        return x
    x = x.reshape(groups // 2, 2, rows, width)
    return jnp.transpose(x, (0, 2, 1, 3)).reshape(groups // 2, rows, 2 * width)


def on_device(
    coeffs_t,
    alpha_table,
    alpha_blocks,
    alpha_types,
    beta_table,
    beta_blocks,
    beta_types,
    row_counts,
):
    groups = lax.axis_size("col")
    rows = coeffs_t.shape[1]
    capacity = 3 * rows // (2 * groups)
    block = rows // alpha_blocks.shape[0]
    starts = (jnp.cumsum(row_counts) - row_counts).astype(jnp.int32)
    keep = lax.dynamic_slice(row_counts, (lax.axis_index("col"),), (1,))

    coeff_slots = slots_call(coeffs_t, starts, groups, capacity, ROW_PARTS)
    types = alpha_entries(alpha_blocks, alpha_types, alpha_table.shape[0])
    a_high, a_low = alpha_rows_call(
        starts, types, *alpha_weights(alpha_table, block), rows, groups, capacity, block
    )
    own, partner, alpha = exchange_call(coeff_slots, coeffs_t, a_high, a_low)
    left, right = beta_weights(beta_table, block)
    wide = lambda x: even_wide(x, block)
    return beta_call(
        [wide(x) for x in own],
        [wide(x) for x in partner],
        wide(alpha),
        left,
        right,
        beta_blocks.reshape(-1),
        beta_types.reshape(-1),
        keep,
        block,
    )


def solution(mesh):
    return jax.shard_map(
        on_device,
        mesh=mesh,
        in_specs=(P(("cls", "col"), None), P(), P(), P(), P(), P("cls", None), P("cls", None), P()),
        out_specs=P("col", "cls"),
        check_vma=False,
    )
```
